128 devices in a mesh: dom: 32 (over z, x, core), hid: 4 (over y).
Axes of the slice: x: 4, y: 4, z: 4, core: 2. Of those that a mesh axis runs over, the one named last changes fastest.
Arguments:
- features: bfloat16 [393216, 512], P('dom', 'hid'), may hold values from -6 to 6
- neigh_mean: bfloat16 [393216, 512], P('dom', 'hid'), may hold values from -6 to 6
- pre_relu: bfloat16 [393216, 512], P('dom', 'hid'), may hold values from -6 to 6
- grad_out: bfloat16 [393216, 512], P('dom', 'hid'), may hold values from -6 to 6
- w_self: bfloat16 [512, 512], P('hid'), may hold values from -0.25 to 0.25
- w_neigh: bfloat16 [512, 512], P('hid'), may hold values from -0.25 to 0.25
- adj_tiles: bfloat16 [6144, 128, 128], P('dom'), may hold values from 0 to 8, as said below
- tile_row: int32 [6144], P('dom'), may hold values from 0 to 95
- tile_col: int32 [6144], P('dom'), may hold values from 0 to 95
- tile_owner: int32 [6144, 1], P('dom'), may hold values from 0 to 31; in each aligned block of 192 rows (0 to 191, 192 to 383, ...) at most 12 rows name the same one
- in_degree: int32 [393216], P('dom'), may hold values from 16 to 128
Outputs:
- grad_feats: bfloat16 [393216, 512], P('dom', 'hid')
- grad_w_self: float32 [512, 512], P('hid')
- grad_w_neigh: float32 [512, 512], P('hid')
- grad_bias: float32 [512], P('hid')
The draws below stay inside these ranges and needn't reach their ends.
Inputs may be any that keep to these rules, and one draw needn't show every extreme that they name: `tile_owner`: among the tiles of one partition no owner is named more than 12 times, a bound that some block reaches. `adj_tiles`: each entry is 0 or lies between 0.5 and 8.
All inputs are finite; a program needn't handle non-finite values.
Results may differ from the reference program's by a relative error of at most 0.0053.
Values may be sent and summed in bfloat16 or wider, within the bound.
No kernel may reach another device: no remote copies, remote signals or barrier semaphores. Data moves between devices by JAX's collectives and lax.ppermute only.
A program may use at most 192 MiB of HBM per device.

```python
import math
import jax
import jax.numpy as jnp
import numpy as np
from jax import lax

FEAT = 512
UNITS = 512
BLOCK = 128
RB = 96
NT_DEV = 192
CAP = 12
HOSTS = 393216
TILES = 6144
N_DOM = 32


def draw_adj_tiles(key, part):
    key = jax.random.fold_in(key, 7)
    first_key, second_key = jax.random.split(key)
    shape = (TILES, BLOCK, BLOCK)
    present = jax.random.randint(first_key, shape, 0, 2).astype(jnp.float32)
    weight = jnp.exp(jax.random.uniform(second_key, shape, jnp.float32, math.log(0.5), math.log(8.0)))
    return (present * weight).astype(jnp.bfloat16)


def touch_ends(result, key, smallest, top_value):
    extent = result.shape
    spot = [jax.random.randint(jax.random.fold_in(key, axis), (), 0, extent[axis]) for axis in range(len(extent))]
    result = result.at[tuple(spot)].set(smallest)
    longest = extent.index(max(extent))
    spot[longest] = (spot[longest] + 1) % extent[longest]
    return result.at[tuple(spot)].set(top_value)


def steps_of(rng, shape, shards, smallest, high):
    def one(axis_at, parts):
        steps = jax.random.uniform(jax.random.fold_in(jax.random.fold_in(rng, 6), axis_at), (parts,), jnp.float32, smallest / len(shards), high / len(shards))
        return jnp.repeat(jnp.exp(steps), shape[axis_at] // parts).reshape((-1,) + (1,) * (len(shape) - axis_at - 1))

    gain = one(*shards[0])
    for cut in shards[1:]:
        gain = gain * one(*cut)
    return gain


def shared_out(stream_key, own, number, rows, count, top, bound, slope):
    ranking = jax.random.permutation(stream_key, count)
    packed, common = load_shares(count, rows * top, bound, slope, True), load_shares(count, rows * top, bound, slope, False)
    places = jnp.arange(count)

    def named(sizes, rotation):
        used = int((sizes > 0).sum())
        fixed = max(1, used // 4)
        moved = fixed + (places - fixed + rotation * (used - fixed)) % max(1, count - fixed)
        return jnp.zeros((count,), jnp.int32).at[ranking[jnp.where(places < fixed, places, moved)]].set(jnp.asarray(sizes, jnp.int32))

    sizes = jnp.where(number % 4 == 0, named(packed, number // 4), named(common, number - number // 4 - 1))
    mixed = jax.random.permutation(jax.random.fold_in(own, 3), count)
    source_of, receiver = mixed[0:count // 2 * 2:2], mixed[1:count // 2 * 2:2]
    slack = jnp.minimum(sizes[source_of] - 1, bound - sizes[receiver]) // 2
    slack = jnp.where((source_of == ranking[0]) | (receiver == ranking[0]) | (sizes[receiver] == 0), 0, jnp.maximum(slack, 0))
    moved = jax.random.randint(jax.random.fold_in(own, 4), (count // 2,), 0, 1 << 20) % (slack + 1)
    sizes = sizes.at[source_of].add(-moved).at[receiver].add(moved)
    members = jnp.searchsorted(jnp.cumsum(sizes), jnp.arange(rows * top), side="right").astype(jnp.int32)
    listing = members.reshape(top, rows).T
    listing = listing[jax.random.permutation(jax.random.fold_in(own, 1), rows)]
    rotation = jax.random.randint(jax.random.fold_in(own, 2), (rows, 1), 0, top)
    return jnp.take_along_axis(listing, (jnp.arange(top)[None, :] + rotation) % top, axis=1)


def load_shares(number_of, total, reach, lean, full):
    loads = [(1 << 20) // math.isqrt(standing ** lean) + 1 for standing in range(1, number_of + 1)]
    largest = reach if full else min(reach, max(-(-total // number_of), total * loads[0] // sum(loads)))
    least = 1 if total - largest >= number_of - 1 else 0
    holding, spare = [largest] + [least] * (number_of - 1), total - largest - least * (number_of - 1)
    while spare > 0:
        movable = [i for i in range(1, number_of) if holding[i] < largest] or [i for i in range(1, number_of) if holding[i] < reach]
        whole, budget = sum([loads[i] for i in movable]), spare
        for i in movable:
            addition = min(reach - holding[i], max(1, budget * loads[i] // whole), spare)
            holding[i] = holding[i] + addition
            spare = spare - addition
    return np.array(holding)


def centred(rng, shape, deviation, bound, shards=(), held_as=jnp.bfloat16):
    values = jax.random.normal(rng, shape, jnp.float32) * deviation
    if len(shards) > 0:
        values = steps_of(rng, shape, shards, -0.22, 0.18) * values
    return jnp.clip(values, min=-bound, max=bound).astype(held_as)


def setup_inputs(seed: int = 0) -> dict:
    key_list = jax.random.split(jax.random.key(seed), 12)
    features = centred(key_list[0], (HOSTS, FEAT), 1.0, 6.0, ((0, 32), (1, 4)))
    neigh_mean = centred(key_list[1], (HOSTS, FEAT), 0.7, 6.0, ((0, 32), (1, 4)))
    pre_relu = centred(key_list[2], (HOSTS, UNITS), 1.0, 6.0, ((0, 32), (1, 4)))
    grad_out = centred(key_list[3], (HOSTS, UNITS), 1.0, 6.0, ((0, 32), (1, 4)))
    w_self = centred(key_list[4], (FEAT, UNITS), UNITS ** -0.5, 0.25, ((0, 4),))
    w_neigh = centred(key_list[5], (FEAT, UNITS), UNITS ** -0.5, 0.25, ((0, 4),))
    adj_tiles = draw_adj_tiles(jax.random.fold_in(key_list[11], 71), 0)
    tile_row = touch_ends(jax.random.randint(key_list[7], (TILES,), 0, RB), jax.random.fold_in(key_list[7], 1), 0, RB - 1).astype(jnp.int32)
    tile_col = touch_ends(jax.random.randint(key_list[8], (TILES,), 0, RB), jax.random.fold_in(key_list[8], 1), 0, RB - 1).astype(jnp.int32)
    tile_owner_keys = jax.random.split(jax.random.fold_in(key_list[9], 1), TILES // NT_DEV)
    tile_owner_turns = jax.random.permutation(jax.random.fold_in(key_list[9], 3), TILES // NT_DEV)
    tile_owner = jax.vmap(lambda own, number: shared_out(jax.random.fold_in(key_list[9], 2), own, number, NT_DEV, N_DOM, 1, CAP, 2))(tile_owner_keys, tile_owner_turns).reshape((TILES, 1))
    in_degree = touch_ends(jax.random.randint(key_list[10], (HOSTS,), 16, 129), jax.random.fold_in(key_list[10], 1), 16, 128).astype(jnp.int32)
    return dict(features=features, neigh_mean=neigh_mean, pre_relu=pre_relu, grad_out=grad_out, w_self=w_self, w_neigh=w_neigh, adj_tiles=adj_tiles, tile_row=tile_row, tile_col=tile_col, tile_owner=tile_owner, in_degree=in_degree)


def reference(features, neigh_mean, pre_relu, grad_out, w_self, w_neigh, adj_tiles, tile_row, tile_col, tile_owner, in_degree):
    grad_scale = 1.0 / math.sqrt(HOSTS)
    masked_grad = jnp.where(pre_relu > 0, grad_out, jnp.zeros_like(grad_out))
    grad_w_self = jnp.dot(features.T, masked_grad, preferred_element_type=jnp.float32) * grad_scale
    grad_w_neigh = jnp.dot(neigh_mean.T, masked_grad, preferred_element_type=jnp.float32) * grad_scale
    grad_bias = lax.optimization_barrier(jnp.sum(masked_grad.astype(jnp.float32), axis=0)) * grad_scale
    contract = (((1,), (1,)), ((), ()))
    pushed = lax.dot_general(masked_grad, w_neigh, contract, preferred_element_type=jnp.float32)
    scaled = (pushed / in_degree.astype(jnp.float32)[:, None]).astype(jnp.bfloat16)
    self_term = lax.dot_general(masked_grad, w_self, contract, preferred_element_type=jnp.float32)
    row_blocks = scaled.reshape(N_DOM, RB, BLOCK, FEAT)
    tile_sets = adj_tiles.reshape(N_DOM, NT_DEV, BLOCK, BLOCK)
    row_sets = tile_row.reshape(N_DOM, NT_DEV).astype(jnp.int32)
    col_sets = tile_col.reshape(N_DOM, NT_DEV).astype(jnp.int32)
    owner_sets = tile_owner[:, 0].reshape(N_DOM, NT_DEV).astype(jnp.int32)
    accumulated = jnp.zeros((N_DOM * RB, BLOCK, FEAT), jnp.float32)

    def one_partition(total, inputs):
        part_blocks, part_tiles, rows_here, cols_here, owners_here = inputs
        chosen = part_blocks[rows_here]
        message = jnp.einsum('tij,tif->tjf', part_tiles.astype(jnp.float32), chosen.astype(jnp.float32))
        message = lax.optimization_barrier(message.astype(jnp.bfloat16)).astype(jnp.float32)
        target = owners_here * RB + cols_here
        return (total.at[target].add(message), None)
    accumulated, _ = lax.scan(one_partition, accumulated, (row_blocks, tile_sets, row_sets, col_sets, owner_sets))
    grad_feats = (self_term + accumulated.reshape(HOSTS, FEAT)).astype(jnp.bfloat16)
    return (grad_feats, grad_w_self, grad_w_neigh, grad_bias)
```

```python
import functools
import math

import jax
import jax.numpy as jnp
from jax import lax
from jax.experimental import pallas as pl
from jax.experimental.pallas import tpu as pltpu
from jax.sharding import PartitionSpec as P

BLK = 128
CAP = 12
HEAD = 96
TAIL = BLK - HEAD
MARK = 16
CHUNK = 2048
WROWS = 48
GROUP = 8
SLICES = 3
VMEM = 40 * 1024 * 1024
F32, BF16 = jnp.float32, jnp.bfloat16


def params():
    return pltpu.CompilerParams(
        dimension_semantics=("arbitrary",), vmem_limit_bytes=VMEM
    )


def cost(flops, size):
    return pl.CostEstimate(flops=flops // 1000, bytes_accessed=size // 1000, transcendentals=0)


def lanes(start, size):
    return pl.ds(pl.multiple_of(start, BLK), size)


def message_kernel(tile_ids, row_ids, grad, degree, far, cols, head, tail, rows, tiles, sem):
    step = pl.program_id(0)

    @pl.when(step == 0)
    def _():
        fetch = pltpu.make_async_copy(far, tiles, sem)
        fetch.start()

        def turn(b, carry):
            at = lanes(b * BLK, BLK)
            turned = grad[at, :].T.astype(F32)
            rows[:, at] = (turned * (1.0 / degree[:, at].astype(F32))).astype(BF16)
            return carry

        lax.fori_loop(0, grad.shape[0] // BLK, turn, 0, unroll=8)
        fetch.wait()

    def one(g, carry):
        base = (step * GROUP + g) * CAP
        for k in range(CAP):
            picked = rows[:, lanes(row_ids[base + k] * BLK, BLK)]
            message = jnp.dot(picked, tiles[tile_ids[base + k]], preferred_element_type=F32)
            message = message.astype(BF16)
            head[g, k * HEAD : (k + 1) * HEAD, :] = message[:HEAD]
            tail[g, k * TAIL : (k + 1) * TAIL, :] = message[HEAD:]
        return carry

    lax.fori_loop(0, GROUP, one, 0)
    head[:, CAP * HEAD :, :] = cols[...]


def messages(tile_ids, row_ids, grad, degree, tiles, cols):
    owners, hosts = cols.shape[0], grad.shape[0]
    whole = pl.BlockSpec(memory_space=pltpu.VMEM)

    def group(height):
        return pl.BlockSpec((GROUP, height, BLK), lambda o, *_: (o, 0, 0))

    heights = (CAP * HEAD + MARK, CAP * TAIL)
    return pl.pallas_call(
        message_kernel,
        grid_spec=pltpu.PrefetchScalarGridSpec(
            num_scalar_prefetch=2,
            grid=(owners // GROUP,),
            in_specs=[whole, whole, pl.BlockSpec(memory_space=pl.ANY), group(MARK)],
            out_specs=[group(h) for h in heights],
            scratch_shapes=[
                pltpu.VMEM((BLK, hosts), BF16),
                pltpu.VMEM(tiles.shape, BF16),
                pltpu.SemaphoreType.DMA,
            ],
        ),
        out_shape=[jax.ShapeDtypeStruct((owners, h, BLK), BF16) for h in heights],
        compiler_params=params(),
        cost_estimate=cost(2 * owners * CAP * BLK**3, 21 << 20),
        name="messages",
    )(tile_ids, row_ids, grad, degree, tiles, cols)


def sum_kernel(height, parts, col_ids, place, received, *rest):
    weights, outs, total = rest[: -parts - 1], rest[-parts - 1 : -1], rest[-1]
    step = pl.program_id(0)

    @pl.when(step == 0)
    def _():
        total[...] = jnp.zeros_like(total)

    def one(g, carry):
        base = (step * GROUP + g) * CAP
        for k in range(CAP):
            at = lanes(col_ids[base + k] * BLK, BLK)
            total[:, at] += received[g, k * height : (k + 1) * height, :].astype(F32)
        return carry

    lax.fori_loop(0, GROUP, one, 0)

    @pl.when(step == pl.num_programs(0) - 1)
    def _():
        width = outs[0].shape[1]
        for k, out in enumerate(outs):
            to = lax.rem(place[0] + k, parts)
            out[:height, :] = total[:, lanes(to * width, width)].astype(BF16)
            for weight in weights:
                units = weight.shape[1]
                for i, r in enumerate(range(0, weight.shape[0], WROWS)):
                    piece = weight[r : r + WROWS, :]
                    out[height : height + piece.shape[0], i * units : (i + 1) * units] = piece


def unit_sums(height, col_ids, place, received, blocks, parts, weight=None):
    sources = received.shape[0]
    width = blocks * BLK // parts
    extra = [] if weight is None else [weight]
    shape = (height + WROWS * len(extra), width)
    return pl.pallas_call(
        functools.partial(sum_kernel, height, parts),
        grid_spec=pltpu.PrefetchScalarGridSpec(
            num_scalar_prefetch=2,
            grid=(sources // GROUP,),
            in_specs=[pl.BlockSpec((GROUP, CAP * height, BLK), lambda p, *_: (p, 0, 0))]
            + [pl.BlockSpec(memory_space=pltpu.VMEM)] * len(extra),
            out_specs=[pl.BlockSpec(shape, lambda p, *_: (0, 0))] * parts,
            scratch_shapes=[pltpu.VMEM((height, (blocks + 1) * BLK), F32)],
        ),
        out_shape=[jax.ShapeDtypeStruct(shape, BF16)] * parts,
        compiler_params=params(),
        cost_estimate=cost(sources * CAP * height * BLK, 9 << 20),
        name="unit_sums",
    )(col_ids, place, received, *extra)


def turn_kernel(place, *rest):
    parts = (len(rest) - 3) // 3
    heads, tails, grad = rest[:parts], rest[parts : 2 * parts], rest[2 * parts]
    outs, near, own = rest[2 * parts + 1 : -2], rest[-2], rest[-1]
    units = grad.shape[1]
    chunk = outs[0].shape[0]
    step = pl.program_id(0)

    @pl.when(step == 0)
    def _():
        for k in range(parts):
            sender = heads[(parts - k) % parts]
            rows = [
                sender[HEAD : HEAD + min(WROWS, 2 * BLK - r), i * units : (i + 1) * units]
                for i, r in enumerate(range(0, 2 * BLK, WROWS))
            ]
            both = jnp.concatenate(rows, axis=0)
            own[:, k * BLK : (k + 1) * BLK] = both[BLK:].T
            near[k * BLK : (k + 1) * BLK, :] = both[:BLK]

        for k in range(parts):
            rows = slice(k * BLK, (k + 1) * BLK)
            blocks = [
                near[rows, lanes(lax.rem(place[0] + parts - i, parts) * BLK, BLK)]
                for i in range(parts)
            ]
            near[rows, :] = jnp.concatenate(blocks, axis=1)

    at = lanes(step * chunk, chunk)
    sums = []
    for head, tail in zip(heads, tails):
        sums += [head[:HEAD, at], tail[:, at]]
    turned = jnp.dot(near[...], jnp.concatenate(sums, axis=0), preferred_element_type=F32)
    result = jnp.dot(grad[...], own[...], preferred_element_type=F32)
    for k, out in enumerate(outs):
        part = result[:, k * BLK : (k + 1) * BLK] + turned[k * BLK : (k + 1) * BLK, :].T
        out[...] = part.astype(BF16)


def turn(place, heads, tails, grad):
    parts, width = len(heads), tails[0].shape[1]
    units = grad.shape[1]
    chunk = width // SLICES
    whole = pl.BlockSpec(memory_space=pltpu.VMEM)
    return pl.pallas_call(
        turn_kernel,
        grid_spec=pltpu.PrefetchScalarGridSpec(
            num_scalar_prefetch=1,
            grid=(SLICES,),
            in_specs=[whole] * (2 * parts)
            + [pl.BlockSpec((chunk, units), lambda i, place: (place[0] * SLICES + i, 0))],
            out_specs=[pl.BlockSpec((chunk, BLK), lambda i, *_: (i, 0))] * parts,
            scratch_shapes=[pltpu.VMEM((units, units), BF16)] * 2,
        ),
        out_shape=[jax.ShapeDtypeStruct((width, BLK), BF16)] * parts,
        compiler_params=params(),
        cost_estimate=cost(4 * units * units * width, 10 << 20),
        name="turn",
    )(place, *heads, *tails, grad)


def weight_kernel(place, first, second, grad, out, total, bias):
    step = pl.program_id(0)
    both = jnp.concatenate([first[...], second[...]], axis=1)
    part = lax.dot_general(both, grad[...], (((0,), (0,)), ((), ())), preferred_element_type=F32)
    ones = jnp.ones((8, grad.shape[0]), BF16)
    column = jnp.dot(ones, grad[...], preferred_element_type=F32)

    @pl.when(step == 0)
    def _():
        total[...] = part
        bias[...] = column

    @pl.when(step > 0)
    def _():
        total[...] += part
        bias[...] += column

    @pl.when(step == pl.num_programs(0) - 1)
    def _():
        mine = bias[:, lanes(place[0] * BLK, BLK)]
        quarters = total.shape[1] // BLK
        for o in range(out.shape[0]):
            for q in range(quarters):
                out[o, 8 * q : 8 * q + 8, :] = total[8 * o : 8 * o + 8, BLK * q : BLK * q + BLK]
            out[o, 8 * quarters :, :] = mine


def weight_parts(place, first, second, grad, owners):
    hosts, units = grad.shape
    height = 8 * (units // BLK) + 8
    piece = pl.BlockSpec((CHUNK, BLK), lambda i, *_: (i, 0))
    return pl.pallas_call(
        weight_kernel,
        grid_spec=pltpu.PrefetchScalarGridSpec(
            num_scalar_prefetch=1,
            grid=(hosts // CHUNK,),
            in_specs=[piece, piece, pl.BlockSpec((CHUNK, units), lambda i, *_: (i, 0))],
            out_specs=pl.BlockSpec((owners, height, BLK), lambda i, *_: (0, 0, 0)),
            scratch_shapes=[pltpu.VMEM((2 * BLK, units), F32), pltpu.VMEM((8, units), F32)],
        ),
        out_shape=jax.ShapeDtypeStruct((owners, height, BLK), F32),
        compiler_params=params(),
        cost_estimate=cost(4 * BLK * hosts * units, 19 << 20),
        name="weight_parts",
    )(place, first, second, grad)


def place_kernel(place, *rest):
    pieces, out = rest[:-1], rest[-1]
    for k, piece in enumerate(pieces):

        @pl.when(pl.program_id(0) == k)
        def _():
            out[...] = piece[...]


def place_quarters(place, pieces):
    parts, (width, features) = len(pieces), pieces[0].shape
    return pl.pallas_call(
        place_kernel,
        grid_spec=pltpu.PrefetchScalarGridSpec(
            num_scalar_prefetch=1,
            grid=(parts,),
            in_specs=[pl.BlockSpec(memory_space=pltpu.VMEM)] * parts,
            out_specs=pl.BlockSpec(
                (width, features), lambda k, place: (lax.rem(place[0] + parts - k, parts), 0)
            ),
        ),
        out_shape=jax.ShapeDtypeStruct((parts * width, features), BF16),
        compiler_params=params(),
        cost_estimate=cost(0, 6 << 20),
        name="place_quarters",
    )(place, *pieces)


def exchange(pieces):
    parts = len(pieces)
    moved = [pieces[0]]
    for k in range(1, parts):
        moved.append(lax.ppermute(pieces[k], "hid", [(i, (i + k) % parts) for i in range(parts)]))
    return moved


def swap(array):
    return lax.all_to_all(array, "dom", split_axis=0, concat_axis=0, tiled=True)


def local(
    features,
    neigh_mean,
    pre_relu,
    grad_out,
    w_self,
    w_neigh,
    adj_tiles,
    tile_row,
    tile_col,
    tile_owner,
    in_degree,
):
    owners = lax.axis_size("dom")
    parts = lax.axis_size("hid")
    hosts = features.shape[0]
    blocks = hosts // BLK
    tile_count = adj_tiles.shape[0]
    slots = owners * CAP
    scale = 1.0 / math.sqrt(hosts * owners)
    place = lax.axis_index("hid").astype(jnp.int32).reshape(1)
    degree = in_degree.reshape(1, hosts)

    grad = jnp.where(pre_relu > 0, grad_out, jnp.zeros_like(grad_out))
    full_grad = lax.all_gather(grad, "hid", axis=1, tiled=True)

    owner = tile_owner[:, 0]
    order = jnp.arange(tile_count, dtype=jnp.int32)
    before = (owner[:, None] == owner[None, :]) & (order[None, :] < order[:, None])
    slot = owner * CAP + jnp.sum(before.astype(jnp.int32), axis=1)
    hit = jnp.arange(slots, dtype=jnp.int32)[:, None] == slot[None, :]
    tile_ids = jnp.sum(jnp.where(hit, order[None, :], 0), axis=1)
    row_ids = jnp.sum(jnp.where(hit, tile_row[None, :], 0), axis=1)
    col_ids = blocks + jnp.sum(jnp.where(hit, tile_col[None, :] - blocks, 0), axis=1)
    cols = jnp.pad(
        col_ids.astype(BF16).reshape(owners, 1, CAP), ((0, 0), (0, MARK - 1), (0, BLK - CAP))
    )

    head, tail = messages(tile_ids, row_ids, grad, degree, adj_tiles, cols)
    weights = jnp.concatenate([w_neigh, w_self], axis=0)
    head, tail, place, weights = lax.optimization_barrier((head, tail, place, weights))
    head = swap(head)
    col_ids = head[:, CAP * HEAD, :CAP].astype(jnp.int32).reshape(slots)
    heads = unit_sums(HEAD, col_ids, place, head, blocks, parts, weights)
    heads, tail, full_grad = lax.optimization_barrier((heads, tail, full_grad))
    heads = exchange(heads)
    tails = unit_sums(TAIL, col_ids, place, swap(tail), blocks, parts)
    tails = exchange(tails)

    pieces = weight_parts(place, features, neigh_mean, full_grad, owners)
    quarters = turn(place, heads, tails, full_grad)
    pieces, quarters = lax.optimization_barrier((pieces, quarters))
    quarters = exchange(quarters)
    summed = jnp.sum(swap(pieces), axis=0)
    rows = 8 * parts
    gathered = swap(jnp.broadcast_to(summed[:rows], (owners, rows, BLK)))
    grads = gathered.reshape(owners, parts, 8, BLK).transpose(0, 2, 1, 3)
    grads = grads.reshape(2 * BLK, parts * BLK) * scale
    bias = summed[rows] * scale

    return place_quarters(place, quarters), grads[:BLK], grads[BLK:], bias


def solution(mesh):
    return jax.shard_map(
        local,
        mesh=mesh,
        in_specs=(
            P("dom", "hid"),
            P("dom", "hid"),
            P("dom", "hid"),
            P("dom", "hid"),
            P("hid", None),
            P("hid", None),
            P("dom", None, None),
            P("dom"),
            P("dom"),
            P("dom", None),
            P("dom"),
        ),
        out_specs=(P("dom", "hid"), P("hid", None), P("hid", None), P("hid")),
        check_vma=False,
    )
```

```python
import functools
import math

import jax
import jax.numpy as jnp
from jax import lax
from jax.experimental import pallas as pl
from jax.experimental.pallas import tpu as pltpu
from jax.sharding import PartitionSpec as P

BLK = 128
CAP = 12
HEAD = 96
TAIL = BLK - HEAD
MARK = 16
CHUNK = 2048
GROUP = 8
SLICES = 2
F32, BF16 = jnp.float32, jnp.bfloat16


def params(limit=40):
    return pltpu.CompilerParams(
        dimension_semantics=("arbitrary",), vmem_limit_bytes=limit * 1024 * 1024
    )


def cost(flops, size):
    return pl.CostEstimate(flops=flops // 1000, bytes_accessed=size // 1000, transcendentals=0)


def lanes(start, size):
    return pl.ds(pl.multiple_of(start, BLK), size)


def mask_kernel(pre_relu, grad_out, near, own, out):
    step = pl.program_id(0)

    @pl.when(step < pl.num_programs(0) - 1)
    def _():
        out[...] = jnp.where(pre_relu[...] > 0, grad_out[...], jnp.zeros_like(grad_out))

    @pl.when(step == pl.num_programs(0) - 1)
    def _():
        count = near.shape[1] // BLK
        for i, weight in enumerate((near, own)):
            for q in range(count):
                at = (i * count + q) * BLK
                out[at : at + BLK, :] = weight[:, q * BLK : (q + 1) * BLK]


def masked(pre_relu, grad_out, near, own):
    hosts = grad_out.shape[0]
    extra = 2 * near.shape[1]
    chunk = 2 * extra
    steps = hosts // chunk
    whole = pl.BlockSpec(memory_space=pltpu.VMEM)
    piece = pl.BlockSpec((chunk, BLK), lambda i: (jnp.minimum(i, steps - 1), 0))
    return pl.pallas_call(
        mask_kernel,
        grid=(steps + 1,),
        in_specs=[piece, piece, whole, whole],
        out_specs=pl.BlockSpec((chunk, BLK), lambda i: (i, 0)),
        out_shape=jax.ShapeDtypeStruct((hosts + extra, BLK), BF16),
        compiler_params=params(60),
        cost_estimate=cost(0, 9 << 20),
        name="masked",
    )(pre_relu, grad_out, near, own)


def message_kernel(
    tile_ids, row_ids, far_grad, degree, far_tiles, cols, head, tail, rows, tiles, grad, sems
):
    step = pl.program_id(0)
    pieces = sems.shape[0] - 1
    width = grad.shape[0] // pieces

    @pl.when(step == 0)
    def _():
        fetches = [
            pltpu.make_async_copy(
                far_grad.at[pl.ds(i * width, width), :],
                grad.at[pl.ds(i * width, width), :],
                sems.at[i],
            )
            for i in range(pieces)
        ]
        fetches.append(pltpu.make_async_copy(far_tiles, tiles, sems.at[pieces]))
        for fetch in fetches:
            fetch.start()

        def turn(b, carry):
            at = lanes(b * BLK, BLK)
            turned = grad[at, :].T.astype(F32)
            rows[:, at] = (turned * (1.0 / degree[:, at].astype(F32))).astype(BF16)
            return carry

        blocks = width // BLK
        for i in range(pieces):
            fetches[i].wait()
            lax.fori_loop(i * blocks, (i + 1) * blocks, turn, 0, unroll=8)
        fetches[pieces].wait()

    def one(g, carry):
        base = (step * GROUP + g) * CAP
        for k in range(CAP):
            picked = rows[:, lanes(row_ids[base + k] * BLK, BLK)]
            message = jnp.dot(picked, tiles[tile_ids[base + k]], preferred_element_type=F32)
            message = message.astype(BF16)
            head[g, k * HEAD : (k + 1) * HEAD, :] = message[:HEAD]
            tail[g, k * TAIL : (k + 1) * TAIL, :] = message[HEAD:]
        return carry

    lax.fori_loop(0, GROUP, one, 0)
    head[:, CAP * HEAD :, :] = cols[...]


def messages(tile_ids, row_ids, grad, degree, tiles, cols):
    owners, hosts = cols.shape[0], degree.shape[1]
    whole = pl.BlockSpec(memory_space=pltpu.VMEM)
    far = pl.BlockSpec(memory_space=pltpu.HBM)

    def group(height):
        return pl.BlockSpec((GROUP, height, BLK), lambda o, *_: (o, 0, 0))

    heights = (CAP * HEAD + MARK, CAP * TAIL)
    return pl.pallas_call(
        message_kernel,
        grid_spec=pltpu.PrefetchScalarGridSpec(
            num_scalar_prefetch=2,
            grid=(owners // GROUP,),
            in_specs=[far, whole, far, group(MARK)],
            out_specs=[group(h) for h in heights],
            scratch_shapes=[
                pltpu.VMEM((BLK, hosts), BF16),
                pltpu.VMEM(tiles.shape, BF16),
                pltpu.VMEM((hosts, BLK), BF16),
                pltpu.SemaphoreType.DMA((5,)),
            ],
        ),
        out_shape=[jax.ShapeDtypeStruct((owners, h, BLK), BF16) for h in heights],
        compiler_params=params(60),
        cost_estimate=cost(2 * owners * CAP * BLK**3, 21 << 20),
        name="messages",
    )(tile_ids, row_ids, grad, degree, tiles, cols)


def sum_kernel(height, place, received, *rest):
    parts = 4
    first = height == HEAD
    if not first:
        sent_marks, rest = rest[0], rest[1:]
    outs, rest = rest[:parts], rest[parts:]
    if first:
        marks, total, held, ready, cols, col_sem, in_sems, out_sems, marked = rest
    else:
        total, held, ready, cols, col_sem, in_sems, out_sems = rest
    groups = received.shape[0] // GROUP

    def fetch(g):
        source = received.at[pl.ds(g * GROUP, GROUP), pl.ds(0, CAP * height), :]
        return pltpu.make_async_copy(source, held.at[g % 2], in_sems.at[g % 2])

    if first:
        source = received.at[:, pl.ds(CAP * HEAD, MARK), :]
        copy = pltpu.make_async_copy(source, marked, col_sem)
        copy.start()
        fetch(0).start()
        copy.wait()
        marks[...] = marked[:, 0, :].astype(F32).astype(jnp.int32)
        copy = pltpu.make_async_copy(marks, cols, col_sem)
        copy.start()
    else:
        copy = pltpu.make_async_copy(sent_marks, cols, col_sem)
        copy.start()
        fetch(0).start()
    total[...] = jnp.zeros_like(total)
    copy.wait()
    for g in range(groups):
        if g + 1 < groups:
            fetch(g + 1).start()
        fetch(g).wait()

        def one(i, carry, g=g):
            for k in range(CAP):
                at = lanes(cols[g * GROUP + i, k] * BLK, BLK)
                total[:, at] += held[g % 2, i, k * height : (k + 1) * height, :].astype(F32)
            return carry

        lax.fori_loop(0, GROUP, one, 0)

    width = ready.shape[2]
    copies = []
    for k, out in enumerate(outs):
        to = lax.rem(place[0] + k, parts)
        ready[k, :, :] = total[:, lanes(to * width, width)].astype(BF16)
        copies.append(pltpu.make_async_copy(ready.at[k], out, out_sems.at[k]))
        copies[k].start()
    for copy in copies:
        copy.wait()


def unit_sums(height, place, received, blocks, parts, *sent_marks):
    first = height == HEAD
    sources = received.shape[0]
    width = blocks * BLK // parts
    shape = (height, width)
    far = pl.BlockSpec(memory_space=pltpu.HBM)
    near = pl.BlockSpec(memory_space=pltpu.VMEM)
    marks = jax.ShapeDtypeStruct((sources, BLK), jnp.int32)
    return pl.pallas_call(
        functools.partial(sum_kernel, height),
        grid_spec=pltpu.PrefetchScalarGridSpec(
            num_scalar_prefetch=1,
            grid=(1,),
            in_specs=[far] + [near] * len(sent_marks),
            out_specs=[far] * parts + [near] * first,
            scratch_shapes=[
                pltpu.VMEM((height, (blocks + 1) * BLK), F32),
                pltpu.VMEM((2, GROUP, CAP * height, BLK), BF16),
                pltpu.VMEM((parts,) + shape, BF16),
                pltpu.SMEM(marks.shape, jnp.int32),
                pltpu.SemaphoreType.DMA,
                pltpu.SemaphoreType.DMA((2,)),
                pltpu.SemaphoreType.DMA((parts,)),
            ]
            + [pltpu.VMEM((sources, MARK, BLK), BF16)] * first,
        ),
        out_shape=[jax.ShapeDtypeStruct(shape, BF16)] * parts + [marks] * first,
        compiler_params=params(53 if first else 40),
        cost_estimate=cost(sources * CAP * height * BLK, 9 << 20),
        name="unit_sums",
    )(place, received, *sent_marks)


def turn_kernel(place, *rest):
    parts = (len(rest) - 4) // 3
    heads, tails, (grad, weights) = rest[:parts], rest[parts : 2 * parts], rest[2 * parts :][:2]
    outs, near, own = rest[2 * parts + 2 : -2], rest[-2], rest[-1]
    units = grad.shape[1]
    chunk = outs[0].shape[0]
    step = pl.program_id(0)

    @pl.when(step == 0)
    def _():
        for k in range(parts):
            to = lanes(lax.rem(place[0] + k, parts) * BLK, BLK)
            here = slice(k * BLK, (k + 1) * BLK)
            for i in range(parts):
                sender = lax.rem(place[0] + parts - i, parts) * BLK
                part = slice(i * BLK, (i + 1) * BLK)
                near[here, part] = weights[lanes(sender, BLK), to]
                own[part, here] = weights[units + i * BLK : units + (i + 1) * BLK, to].T

    at = lanes(step * chunk, chunk)
    sums = []
    for head, tail in zip(heads, tails):
        sums += [head[:, at], tail[:, at]]
    turned = jnp.dot(near[...], jnp.concatenate(sums, axis=0), preferred_element_type=F32)
    result = jnp.dot(grad[...], own[...], preferred_element_type=F32)
    for k, out in enumerate(outs):
        part = result[:, k * BLK : (k + 1) * BLK] + turned[k * BLK : (k + 1) * BLK, :].T
        out[...] = part.astype(BF16)


def turn(place, heads, tails, grad):
    parts, width = len(heads), tails[0].shape[1]
    units = grad.shape[1]
    chunk = width // SLICES
    last = grad.shape[0] // (2 * units) - 1
    whole = pl.BlockSpec(memory_space=pltpu.VMEM)
    return pl.pallas_call(
        turn_kernel,
        grid_spec=pltpu.PrefetchScalarGridSpec(
            num_scalar_prefetch=1,
            grid=(SLICES,),
            in_specs=[whole] * (2 * parts)
            + [
                pl.BlockSpec((chunk, units), lambda i, place: (place[0] * SLICES + i, 0)),
                pl.BlockSpec((2 * units, units), lambda i, *_: (last, 0)),
            ],
            out_specs=[pl.BlockSpec((chunk, BLK), lambda i, *_: (i, 0))] * parts,
            scratch_shapes=[pltpu.VMEM((units, units), BF16)] * 2,
        ),
        out_shape=[jax.ShapeDtypeStruct((width, BLK), BF16)] * parts,
        compiler_params=params(),
        cost_estimate=cost(4 * units * units * width, 10 << 20),
        name="turn",
    )(place, *heads, *tails, grad, grad)


def weight_kernel(place, first, second, grad, out, total, bias):
    step = pl.program_id(0)
    both = jnp.concatenate([first[...], second[...]], axis=1)
    part = lax.dot_general(both, grad[...], (((0,), (0,)), ((), ())), preferred_element_type=F32)
    ones = jnp.ones((8, grad.shape[0]), BF16)
    column = jnp.dot(ones, grad[...], preferred_element_type=F32)

    @pl.when(step == 0)
    def _():
        total[...] = part
        bias[...] = column

    @pl.when(step > 0)
    def _():
        total[...] += part
        bias[...] += column

    @pl.when(step == pl.num_programs(0) - 1)
    def _():
        mine = bias[:, lanes(place[0] * BLK, BLK)]
        quarters = total.shape[1] // BLK
        for o in range(out.shape[0]):
            for q in range(quarters):
                out[o, 8 * q : 8 * q + 8, :] = total[8 * o : 8 * o + 8, BLK * q : BLK * q + BLK]
            out[o, 8 * quarters :, :] = mine


def weight_parts(place, first, second, grad, owners):
    hosts, units = first.shape[0], grad.shape[1]
    height = 8 * (units // BLK) + 8
    piece = pl.BlockSpec((CHUNK, BLK), lambda i, *_: (i, 0))
    return pl.pallas_call(
        weight_kernel,
        grid_spec=pltpu.PrefetchScalarGridSpec(
            num_scalar_prefetch=1,
            grid=(hosts // CHUNK,),
            in_specs=[piece, piece, pl.BlockSpec((CHUNK, units), lambda i, *_: (i, 0))],
            out_specs=pl.BlockSpec((owners, height, BLK), lambda i, *_: (0, 0, 0)),
            scratch_shapes=[pltpu.VMEM((2 * BLK, units), F32), pltpu.VMEM((8, units), F32)],
        ),
        out_shape=jax.ShapeDtypeStruct((owners, height, BLK), F32),
        compiler_params=params(),
        cost_estimate=cost(4 * BLK * hosts * units, 19 << 20),
        name="weight_parts",
    )(place, first, second, grad)


def place_kernel(place, *rest):
    pieces, out = rest[:-1], rest[-1]
    for k, piece in enumerate(pieces):

        @pl.when(pl.program_id(0) == k)
        def _():
            out[...] = piece[...]


def place_quarters(place, pieces):
    parts, (width, features) = len(pieces), pieces[0].shape
    return pl.pallas_call(
        place_kernel,
        grid_spec=pltpu.PrefetchScalarGridSpec(
            num_scalar_prefetch=1,
            grid=(parts,),
            in_specs=[pl.BlockSpec(memory_space=pltpu.VMEM)] * parts,
            out_specs=pl.BlockSpec(
                (width, features), lambda k, place: (lax.rem(place[0] + parts - k, parts), 0)
            ),
        ),
        out_shape=jax.ShapeDtypeStruct((parts * width, features), BF16),
        compiler_params=params(),
        cost_estimate=cost(0, 6 << 20),
        name="place_quarters",
    )(place, *pieces)


def exchange(pieces):
    parts = len(pieces)
    moved = [pieces[0]]
    for k in range(1, parts):
        moved.append(lax.ppermute(pieces[k], "hid", [(i, (i + k) % parts) for i in range(parts)]))
    return moved


def swap(array):
    return lax.all_to_all(array, "dom", split_axis=0, concat_axis=0, tiled=True)


def local(
    features,
    neigh_mean,
    pre_relu,
    grad_out,
    w_self,
    w_neigh,
    adj_tiles,
    tile_row,
    tile_col,
    tile_owner,
    in_degree,
):
    owners = lax.axis_size("dom")
    parts = lax.axis_size("hid")
    hosts = features.shape[0]
    blocks = hosts // BLK
    tile_count = adj_tiles.shape[0]
    slots = owners * CAP
    scale = 1.0 / math.sqrt(hosts * owners)
    place = lax.axis_index("hid").astype(jnp.int32).reshape(1)
    degree = in_degree.reshape(1, hosts)

    grad = masked(pre_relu, grad_out, w_neigh, w_self)
    full_grad = lax.all_gather(grad, "hid", axis=1, tiled=True)

    owner = tile_owner[:, 0]
    order = jnp.arange(tile_count, dtype=jnp.int32)
    before = (owner[:, None] == owner[None, :]) & (order[None, :] < order[:, None])
    slot = owner * CAP + jnp.sum(before.astype(jnp.int32), axis=1)
    hit = jnp.arange(slots, dtype=jnp.int32)[:, None] == slot[None, :]
    tile_ids = jnp.sum(jnp.where(hit, order[None, :], 0), axis=1)
    row_ids = jnp.sum(jnp.where(hit, tile_row[None, :], 0), axis=1)
    col_ids = blocks + jnp.sum(jnp.where(hit, tile_col[None, :] - blocks, 0), axis=1)
    cols = jnp.pad(
        col_ids.astype(BF16).reshape(owners, 1, CAP), ((0, 0), (0, MARK - 1), (0, BLK - CAP))
    )

    head, tail = messages(tile_ids, row_ids, grad, degree, adj_tiles, cols)
    head, tail, place = lax.optimization_barrier((head, tail, place))
    head, tail = lax.optimization_barrier((swap(head), tail))
    tail = swap(tail)
    *heads, marks = unit_sums(HEAD, place, head, blocks, parts)
    heads, full_grad = lax.optimization_barrier((heads, full_grad))
    heads = exchange(heads)
    pieces = weight_parts(place, features, neigh_mean, full_grad, owners)
    tail, pieces, heads = lax.optimization_barrier((tail, pieces, heads))
    tails = unit_sums(TAIL, place, tail, blocks, parts, marks)
    quarters = turn(place, heads, exchange(tails), full_grad)
    pieces, quarters = lax.optimization_barrier((pieces, quarters))
    quarters = exchange(quarters)
    summed = jnp.sum(swap(pieces), axis=0)
    rows = 8 * parts
    summed, quarters[2] = lax.optimization_barrier((summed, quarters[2]))
    gathered = swap(jnp.broadcast_to(summed[:rows], (owners, rows, BLK)))
    grads = gathered.reshape(owners, parts, 8, BLK).transpose(0, 2, 1, 3)
    grads = grads.reshape(2 * BLK, parts * BLK) * scale
    bias = summed[rows] * scale
    quarters, grads, bias = lax.optimization_barrier((quarters, grads, bias))

    return place_quarters(place, quarters), grads[:BLK], grads[BLK:], bias


def solution(mesh):
    return jax.shard_map(
        local,
        mesh=mesh,
        in_specs=(
            P("dom", "hid"),
            P("dom", "hid"),
            P("dom", "hid"),
            P("dom", "hid"),
            P("hid", None),
            P("hid", None),
            P("dom", None, None),
            P("dom"),
            P("dom"),
            P("dom", None),
            P("dom"),
        ),
        out_specs=(P("dom", "hid"), P("hid", None), P("hid", None), P("hid")),
        check_vma=False,
    )
```

```python
import functools
import math

import jax
import jax.numpy as jnp
from jax import lax
from jax.experimental import pallas as pl
from jax.experimental.pallas import tpu as pltpu
from jax.sharding import PartitionSpec as P

BLK = 128
CAP = 12
HEAD = 96
TAIL = BLK - HEAD
MARK = 16
CHUNK = 2048
GROUP = 8
SLICES = 2
F32, BF16 = jnp.float32, jnp.bfloat16


def params(limit=40):
    return pltpu.CompilerParams(
        dimension_semantics=("arbitrary",), vmem_limit_bytes=limit * 1024 * 1024
    )


def cost(flops, size):
    return pl.CostEstimate(flops=flops // 1000, bytes_accessed=size // 1000, transcendentals=0)


def lanes(start, size):
    return pl.ds(pl.multiple_of(start, BLK), size)


def mask_kernel(pre_relu, grad_out, near, own, out):
    step = pl.program_id(0)

    @pl.when(step < pl.num_programs(0) - 1)
    def _():
        out[...] = jnp.where(pre_relu[...] > 0, grad_out[...], jnp.zeros_like(grad_out))

    @pl.when(step == pl.num_programs(0) - 1)
    def _():
        count = near.shape[1] // BLK
        for i, weight in enumerate((near, own)):
            for q in range(count):
                at = (i * count + q) * BLK
                out[at : at + BLK, :] = weight[:, q * BLK : (q + 1) * BLK]


def masked(pre_relu, grad_out, near, own):
    hosts = grad_out.shape[0]
    extra = 2 * near.shape[1]
    chunk = 4 * extra
    steps = hosts // chunk
    whole = pl.BlockSpec(memory_space=pltpu.VMEM)
    piece = pl.BlockSpec((chunk, BLK), lambda i: (jnp.minimum(i, steps - 1), 0))
    return pl.pallas_call(
        mask_kernel,
        grid=(steps + 1,),
        in_specs=[piece, piece, whole, whole],
        out_specs=pl.BlockSpec((chunk, BLK), lambda i: (i, 0)),
        out_shape=jax.ShapeDtypeStruct((hosts + extra, BLK), BF16),
        compiler_params=params(60),
        cost_estimate=cost(0, 9 << 20),
        name="masked",
    )(pre_relu, grad_out, near, own)


def message_kernel(
    tile_ids, row_ids, far_grad, degree, far_tiles, cols, head, tail, rows, tiles, grad, sems
):
    step = pl.program_id(0)
    pieces = sems.shape[0] - 1
    width = grad.shape[0] // pieces

    @pl.when(step == 0)
    def _():
        fetches = [
            pltpu.make_async_copy(
                far_grad.at[pl.ds(i * width, width), :],
                grad.at[pl.ds(i * width, width), :],
                sems.at[i],
            )
            for i in range(pieces)
        ]
        fetches.append(pltpu.make_async_copy(far_tiles, tiles, sems.at[pieces]))
        for fetch in fetches:
            fetch.start()

        def turn(b, carry):
            at = lanes(b * BLK, BLK)
            turned = grad[at, :].T.astype(F32)
            rows[:, at] = (turned * (1.0 / degree[:, at].astype(F32))).astype(BF16)
            return carry

        blocks = width // BLK
        for i in range(pieces):
            fetches[i].wait()
            lax.fori_loop(i * blocks, (i + 1) * blocks, turn, 0, unroll=8)
        fetches[pieces].wait()

    def one(g, carry):
        base = (step * GROUP + g) * CAP
        for k in range(CAP):
            picked = rows[:, lanes(row_ids[base + k] * BLK, BLK)]
            message = jnp.dot(picked, tiles[tile_ids[base + k]], preferred_element_type=F32)
            message = message.astype(BF16)
            head[g, k * HEAD : (k + 1) * HEAD, :] = message[:HEAD]
            tail[g, k * TAIL : (k + 1) * TAIL, :] = message[HEAD:]
        return carry

    lax.fori_loop(0, GROUP, one, 0)
    head[:, CAP * HEAD :, :] = cols[...]


def messages(tile_ids, row_ids, grad, degree, tiles, cols):
    owners, hosts = cols.shape[0], degree.shape[1]
    whole = pl.BlockSpec(memory_space=pltpu.VMEM)
    far = pl.BlockSpec(memory_space=pltpu.HBM)

    def group(height):
        return pl.BlockSpec((GROUP, height, BLK), lambda o, *_: (o, 0, 0))

    heights = (CAP * HEAD + MARK, CAP * TAIL)
    return pl.pallas_call(
        message_kernel,
        grid_spec=pltpu.PrefetchScalarGridSpec(
            num_scalar_prefetch=2,
            grid=(owners // GROUP,),
            in_specs=[far, whole, far, group(MARK)],
            out_specs=[group(h) for h in heights],
            scratch_shapes=[
                pltpu.VMEM((BLK, hosts), BF16),
                pltpu.VMEM(tiles.shape, BF16),
                pltpu.VMEM((hosts, BLK), BF16),
                pltpu.SemaphoreType.DMA((5,)),
            ],
        ),
        out_shape=[jax.ShapeDtypeStruct((owners, h, BLK), BF16) for h in heights],
        compiler_params=params(60),
        cost_estimate=cost(2 * owners * CAP * BLK**3, 21 << 20),
        name="messages",
    )(tile_ids, row_ids, grad, degree, tiles, cols)


def sum_kernel(height, place, received, *rest):
    parts = 4
    first = height == HEAD
    if not first:
        sent_marks, rest = rest[0], rest[1:]
    outs, rest = rest[:parts], rest[parts:]
    if first:
        marks, total, held, ready, cols, col_sem, in_sems, out_sems, marked = rest
    else:
        total, held, ready, cols, col_sem, in_sems, out_sems = rest
    groups = received.shape[0] // GROUP

    def fetch(g):
        source = received.at[pl.ds(g * GROUP, GROUP), pl.ds(0, CAP * height), :]
        return pltpu.make_async_copy(source, held.at[g % 2], in_sems.at[g % 2])

    if first:
        source = received.at[:, pl.ds(CAP * HEAD, MARK), :]
        copy = pltpu.make_async_copy(source, marked, col_sem)
        copy.start()
        fetch(0).start()
        copy.wait()
        marks[...] = marked[:, 0, :].astype(F32).astype(jnp.int32)
        copy = pltpu.make_async_copy(marks, cols, col_sem)
        copy.start()
    else:
        copy = pltpu.make_async_copy(sent_marks, cols, col_sem)
        copy.start()
        fetch(0).start()
    total[...] = jnp.zeros_like(total)
    copy.wait()
    for g in range(groups):
        if g + 1 < groups:
            fetch(g + 1).start()
        fetch(g).wait()

        def one(i, carry, g=g):
            for k in range(CAP):
                at = lanes(cols[g * GROUP + i, k] * BLK, BLK)
                total[:, at] += held[g % 2, i, k * height : (k + 1) * height, :].astype(F32)
            return carry

        lax.fori_loop(0, GROUP, one, 0)

    width = ready.shape[2]
    copies = []
    for k, out in enumerate(outs):
        to = lax.rem(place[0] + k, parts)
        ready[k, :, :] = total[:, lanes(to * width, width)].astype(BF16)
        copies.append(pltpu.make_async_copy(ready.at[k], out, out_sems.at[k]))
        copies[k].start()
    for copy in copies:
        copy.wait()


def unit_sums(height, place, received, blocks, parts, *sent_marks):
    first = height == HEAD
    sources = received.shape[0]
    width = blocks * BLK // parts
    shape = (height, width)
    far = pl.BlockSpec(memory_space=pltpu.HBM)
    near = pl.BlockSpec(memory_space=pltpu.VMEM)
    marks = jax.ShapeDtypeStruct((sources, BLK), jnp.int32)
    return pl.pallas_call(
        functools.partial(sum_kernel, height),
        grid_spec=pltpu.PrefetchScalarGridSpec(
            num_scalar_prefetch=1,
            grid=(1,),
            in_specs=[far] + [near] * len(sent_marks),
            out_specs=[far] * parts + [near] * first,
            scratch_shapes=[
                pltpu.VMEM((height, (blocks + 1) * BLK), F32),
                pltpu.VMEM((2, GROUP, CAP * height, BLK), BF16),
                pltpu.VMEM((parts,) + shape, BF16),
                pltpu.SMEM(marks.shape, jnp.int32),
                pltpu.SemaphoreType.DMA,
                pltpu.SemaphoreType.DMA((2,)),
                pltpu.SemaphoreType.DMA((parts,)),
            ]
            + [pltpu.VMEM((sources, MARK, BLK), BF16)] * first,
        ),
        out_shape=[jax.ShapeDtypeStruct(shape, BF16)] * parts + [marks] * first,
        compiler_params=params(53 if first else 40),
        cost_estimate=cost(sources * CAP * height * BLK, 9 << 20),
        name="unit_sums",
    )(place, received, *sent_marks)


def turn_kernel(place, *rest):
    parts = (len(rest) - 4) // 3
    heads, tails, (grad, weights) = rest[:parts], rest[parts : 2 * parts], rest[2 * parts :][:2]
    outs, near, own = rest[2 * parts + 2 : -2], rest[-2], rest[-1]
    units = grad.shape[1]
    chunk = outs[0].shape[0]
    step = pl.program_id(0)

    @pl.when(step == 0)
    def _():
        for k in range(parts):
            to = lanes(lax.rem(place[0] + k, parts) * BLK, BLK)
            here = slice(k * BLK, (k + 1) * BLK)
            for i in range(parts):
                sender = lax.rem(place[0] + parts - i, parts) * BLK
                part = slice(i * BLK, (i + 1) * BLK)
                near[part, here] = weights[lanes(sender, BLK), to].T
                own[part, here] = weights[units + i * BLK : units + (i + 1) * BLK, to].T

    at = lanes(step * chunk, chunk)
    sums = []
    for head, tail in zip(heads, tails):
        sums += [head[:, at], tail[:, at]]
    result = jnp.dot(grad[...], own[...], preferred_element_type=F32) + lax.dot_general(
        jnp.concatenate(sums, axis=0),
        near[...],
        (((0,), (0,)), ((), ())),
        preferred_element_type=F32,
    )
    for k, out in enumerate(outs):
        out[...] = result[:, k * BLK : (k + 1) * BLK].astype(BF16)


def turn(place, heads, tails, grad):
    parts, width = len(heads), tails[0].shape[1]
    units = grad.shape[1]
    chunk = width // SLICES
    last = grad.shape[0] // (2 * units) - 1
    whole = pl.BlockSpec(memory_space=pltpu.VMEM)
    return pl.pallas_call(
        turn_kernel,
        grid_spec=pltpu.PrefetchScalarGridSpec(
            num_scalar_prefetch=1,
            grid=(SLICES,),
            in_specs=[whole] * (2 * parts)
            + [
                pl.BlockSpec((chunk, units), lambda i, place: (place[0] * SLICES + i, 0)),
                pl.BlockSpec((2 * units, units), lambda i, *_: (last, 0)),
            ],
            out_specs=[pl.BlockSpec((chunk, BLK), lambda i, *_: (i, 0))] * parts,
            scratch_shapes=[pltpu.VMEM((units, units), BF16)] * 2,
        ),
        out_shape=[jax.ShapeDtypeStruct((width, BLK), BF16)] * parts,
        compiler_params=params(),
        cost_estimate=cost(4 * units * units * width, 10 << 20),
        name="turn",
    )(place, *heads, *tails, grad, grad)


def weight_kernel(place, first, second, grad, out, total, bias):
    step = pl.program_id(0)
    both = jnp.concatenate([first[...], second[...]], axis=1)
    part = lax.dot_general(both, grad[...], (((0,), (0,)), ((), ())), preferred_element_type=F32)
    ones = jnp.ones((8, grad.shape[0]), BF16)
    column = jnp.dot(ones, grad[...], preferred_element_type=F32)

    @pl.when(step == 0)
    def _():
        total[...] = part
        bias[...] = column

    @pl.when(step > 0)
    def _():
        total[...] += part
        bias[...] += column

    @pl.when(step == pl.num_programs(0) - 1)
    def _():
        mine = bias[:, lanes(place[0] * BLK, BLK)]
        quarters = total.shape[1] // BLK
        for o in range(out.shape[0]):
            for q in range(quarters):
                out[o, 8 * q : 8 * q + 8, :] = total[8 * o : 8 * o + 8, BLK * q : BLK * q + BLK]
            out[o, 8 * quarters :, :] = mine


def weight_parts(place, first, second, grad, owners):
    hosts, units = first.shape[0], grad.shape[1]
    height = 8 * (units // BLK) + 8
    piece = pl.BlockSpec((CHUNK, BLK), lambda i, *_: (i, 0))
    return pl.pallas_call(
        weight_kernel,
        grid_spec=pltpu.PrefetchScalarGridSpec(
            num_scalar_prefetch=1,
            grid=(hosts // CHUNK,),
            in_specs=[piece, piece, pl.BlockSpec((CHUNK, units), lambda i, *_: (i, 0))],
            out_specs=pl.BlockSpec((owners, height, BLK), lambda i, *_: (0, 0, 0)),
            scratch_shapes=[pltpu.VMEM((2 * BLK, units), F32), pltpu.VMEM((8, units), F32)],
        ),
        out_shape=jax.ShapeDtypeStruct((owners, height, BLK), F32),
        compiler_params=params(),
        cost_estimate=cost(4 * BLK * hosts * units, 19 << 20),
        name="weight_parts",
    )(place, first, second, grad)


def place_kernel(place, *rest):
    pieces, out = rest[:-1], rest[-1]
    for k, piece in enumerate(pieces):

        @pl.when(pl.program_id(0) == k)
        def _():
            out[...] = piece[...]


def place_quarters(place, pieces):
    parts, (width, features) = len(pieces), pieces[0].shape
    return pl.pallas_call(
        place_kernel,
        grid_spec=pltpu.PrefetchScalarGridSpec(
            num_scalar_prefetch=1,
            grid=(parts,),
            in_specs=[pl.BlockSpec(memory_space=pltpu.VMEM)] * parts,
            out_specs=pl.BlockSpec(
                (width, features), lambda k, place: (lax.rem(place[0] + parts - k, parts), 0)
            ),
        ),
        out_shape=jax.ShapeDtypeStruct((parts * width, features), BF16),
        compiler_params=params(),
        cost_estimate=cost(0, 6 << 20),
        name="place_quarters",
    )(place, *pieces)


def exchange(pieces):
    parts = len(pieces)
    moved = [pieces[0]]
    for k in range(1, parts):
        moved.append(lax.ppermute(pieces[k], "hid", [(i, (i + k) % parts) for i in range(parts)]))
    return moved


def swap(array):
    return lax.all_to_all(array, "dom", split_axis=0, concat_axis=0, tiled=True)


def local(
    features,
    neigh_mean,
    pre_relu,
    grad_out,
    w_self,
    w_neigh,
    adj_tiles,
    tile_row,
    tile_col,
    tile_owner,
    in_degree,
):
    owners = lax.axis_size("dom")
    parts = lax.axis_size("hid")
    hosts = features.shape[0]
    blocks = hosts // BLK
    tile_count = adj_tiles.shape[0]
    slots = owners * CAP
    scale = 1.0 / math.sqrt(hosts * owners)
    place = lax.axis_index("hid").astype(jnp.int32).reshape(1)
    degree = in_degree.reshape(1, hosts)

    grad = masked(pre_relu, grad_out, w_neigh, w_self)
    full_grad = lax.all_gather(grad, "hid", axis=1, tiled=True)

    owner = tile_owner[:, 0]
    order = jnp.arange(tile_count, dtype=jnp.int32)
    before = (owner[:, None] == owner[None, :]) & (order[None, :] < order[:, None])
    slot = owner * CAP + jnp.sum(before.astype(jnp.int32), axis=1)
    hit = jnp.arange(slots, dtype=jnp.int32)[:, None] == slot[None, :]
    tile_ids = jnp.sum(jnp.where(hit, order[None, :], 0), axis=1)
    row_ids = jnp.sum(jnp.where(hit, tile_row[None, :], 0), axis=1)
    col_ids = blocks + jnp.sum(jnp.where(hit, tile_col[None, :] - blocks, 0), axis=1)
    cols = jnp.pad(
        col_ids.astype(BF16).reshape(owners, 1, CAP), ((0, 0), (0, MARK - 1), (0, BLK - CAP))
    )

    head, tail = messages(tile_ids, row_ids, grad, degree, adj_tiles, cols)
    head, tail, place = lax.optimization_barrier((head, tail, place))
    head, tail = lax.optimization_barrier((swap(head), tail))
    tail = swap(tail)
    *heads, marks = unit_sums(HEAD, place, head, blocks, parts)
    heads, full_grad = lax.optimization_barrier((heads, full_grad))
    heads = exchange(heads)
    pieces = weight_parts(place, features, neigh_mean, full_grad, owners)
    tail, pieces, heads = lax.optimization_barrier((tail, pieces, heads))
    tails = unit_sums(TAIL, place, tail, blocks, parts, marks)
    tails = exchange(tails)
    tails[2], pieces = lax.optimization_barrier((tails[2], pieces))
    quarters = turn(place, heads, tails, full_grad)
    quarters = exchange(quarters)
    summed = jnp.sum(swap(pieces), axis=0)
    rows = 8 * parts
    summed, quarters[2] = lax.optimization_barrier((summed, quarters[2]))
    gathered = swap(jnp.broadcast_to(summed[:rows], (owners, rows, BLK)))
    grads = gathered.reshape(owners, parts, 8, BLK).transpose(0, 2, 1, 3)
    grads = grads.reshape(2 * BLK, parts * BLK) * scale
    bias = summed[rows] * scale
    quarters, grads, bias = lax.optimization_barrier((quarters, grads, bias))

    return place_quarters(place, quarters), grads[:BLK], grads[BLK:], bias


def solution(mesh):
    return jax.shard_map(
        local,
        mesh=mesh,
        in_specs=(
            P("dom", "hid"),
            P("dom", "hid"),
            P("dom", "hid"),
            P("dom", "hid"),
            P("hid", None),
            P("hid", None),
            P("dom", None, None),
            P("dom"),
            P("dom"),
            P("dom", None),
            P("dom"),
        ),
        out_specs=(P("dom", "hid"), P("hid", None), P("hid", None), P("hid")),
        check_vma=False,
    )
```
